32 devices in a mesh: member: 2 (over y), row: 4 (over z), col: 4 (over x, core).
Axes of the slice: x: 2, y: 2, z: 4, core: 2. Of those that a mesh axis runs over, the one named last changes fastest.
Arguments:
- tokens: bfloat16 [128, 8192], P(('member', 'row'), 'col'), parts along dimension 0, may hold values from -6 to 6
- output_grad: bfloat16 [128, 8192], P(('member', 'row'), 'col'), parts along dimension 0, may hold values from -6 to 6
- gate_weight: bfloat16 [32768, 8192], P(('member', 'row'), 'col'), parts along dimension 0, may hold values from -0.09375 to 0.09375
- up_weight: bfloat16 [32768, 8192], P(('member', 'row'), 'col'), parts along dimension 0, may hold values from -0.09375 to 0.09375
- down_weight: bfloat16 [16384, 16384], P(('member', 'col'), 'row'), parts along dimension 0, may hold values from -0.0625 to 0.0625
- gate_mask: int32 [128, 64], P('row', 'col'), may hold values from 0 to 1, as said below
- up_mask: int32 [128, 64], P('row', 'col'), may hold values from 0 to 1, as said below
- down_mask: int32 [64, 128], P('col', 'row'), may hold values from 0 to 1, as said below
Outputs:
- output: bfloat16 [128, 8192], P(('member', 'row'), 'col'), parts along dimension 0
- input_grad: bfloat16 [128, 8192], P(('member', 'row'), 'col'), parts along dimension 0
- gate_grad: bfloat16 [32768, 8192], P(('member', 'row'), 'col'), parts along dimension 0
- up_grad: bfloat16 [32768, 8192], P(('member', 'row'), 'col'), parts along dimension 0
- down_grad: bfloat16 [16384, 16384], P(('member', 'col'), 'row'), parts along dimension 0
The draws below stay inside these ranges and needn't reach their ends.
There are 2 independent parts, one for each index of `member`. The reference program is written for one: setup_inputs(seed, part) draws one part's arguments, and reference() takes and returns one part's arrays. A program takes and returns all parts, laid end to end along the dimension named above; an argument that names none is the same for every part. Nothing has to cross between parts.
Inputs may be any that keep to these rules, and one draw needn't show every extreme that they name: `gate_mask`: each entry is 0 (block pruned) or 1 (block kept); the share of kept blocks differs between regions of the matrix. `up_mask`: each entry is 0 (block pruned) or 1 (block kept); the share of kept blocks differs between regions of the matrix. `down_mask`: each entry is 0 (block pruned) or 1 (block kept); the share of kept blocks differs between regions of the matrix.
All inputs are finite; a program needn't handle non-finite values.
Results may differ from the reference program's by a relative error of at most 0.017.
Values may be sent and summed in bfloat16 or wider, within the bound.
No kernel may reach another device: no remote copies, remote signals or barrier semaphores. Data moves between devices by JAX's collectives and lax.ppermute only.
A program may use at most 320 MiB of HBM per device.

```python
import jax
import jax.numpy as jnp

D = 8192
FF = 16384
BLOCK = 128
TOKENS = 64


def block_pattern(key, shape, coarse):
    level_key, pick_key = jax.random.split(key)
    level = jax.random.randint(level_key, coarse, 2, 7)
    level = jnp.repeat(jnp.repeat(level, shape[0] // coarse[0], axis=0), shape[1] // coarse[1], axis=1)
    picked = jax.random.randint(pick_key, shape, 0, 8)
    return jnp.where(picked < level, 1, 0).astype(jnp.int32)


def draw_gate_mask(key, part):
    key = jax.random.fold_in(key, 11)
    return block_pattern(key, (FF // BLOCK, D // BLOCK), (8, 4))


def draw_up_mask(key, part):
    key = jax.random.fold_in(key, 12)
    return block_pattern(key, (FF // BLOCK, D // BLOCK), (8, 4))


def draw_down_mask(key, part):
    key = jax.random.fold_in(key, 13)
    return block_pattern(key, (D // BLOCK, FF // BLOCK), (4, 8))


def block_scale(key, shape, cuts, smallest, high):
    level = 1.0
    for dim, parts in cuts:
        heights = jax.random.uniform(jax.random.fold_in(jax.random.fold_in(key, 6), dim), (parts,), jnp.float32, smallest / len(cuts), high / len(cuts))
        level = level * jnp.repeat(jnp.exp(heights), shape[dim] // parts).reshape((-1,) + (1,) * (len(shape) - 1 - dim))
    return level


def normal_values(key, extent, deviation, bound, pieces=(), kind=jnp.bfloat16):
    drawn = jax.random.normal(key, extent, jnp.float32) * deviation
    if len(pieces) > 0:
        drawn = block_scale(key, extent, pieces, -0.22, 0.18) * drawn
    return jnp.clip(drawn, min=-bound, max=bound).astype(kind)


def setup_inputs(seed: int = 0, part: int = 0) -> dict:
    seeds = jax.random.split(jax.random.key(seed), 9)
    part_splits = jax.random.split(jax.random.fold_in(seeds[8], part), 9)
    tokens = normal_values(part_splits[0], (TOKENS, D), 1.0, 6.0, ((0, 4), (1, 4)))
    output_grad = normal_values(part_splits[1], (TOKENS, D), 1.0, 6.0, ((0, 4), (1, 4)))
    gate_weight = normal_values(part_splits[2], (FF, D), (D // 2) ** -0.5, 0.09375, ((0, 4), (1, 4)))
    up_weight = normal_values(part_splits[3], (FF, D), (D // 2) ** -0.5, 0.09375, ((0, 4), (1, 4)))
    down_weight = normal_values(part_splits[4], (D, FF), (FF // 2) ** -0.5, 0.0625, ((0, 4), (1, 4)))
    gate_mask = draw_gate_mask(jax.random.fold_in(seeds[8], 71), part)
    up_mask = draw_up_mask(jax.random.fold_in(seeds[8], 71), part)
    down_mask = draw_down_mask(jax.random.fold_in(seeds[8], 71), part)
    return {"tokens": tokens, "output_grad": output_grad, "gate_weight": gate_weight, "up_weight": up_weight, "down_weight": down_weight, "gate_mask": gate_mask, "up_mask": up_mask, "down_mask": down_mask}


def widen(weight, block_mask):
    num_rows, num_cols = weight.shape
    mask_rows, mask_cols = block_mask.shape
    shaped = weight.reshape(mask_rows, num_rows // mask_rows, mask_cols, num_cols // mask_cols)
    shaped = shaped * block_mask[:, None, :, None].astype(weight.dtype)
    return shaped.reshape(num_rows, num_cols)


def reference(tokens, output_grad, gate_weight, up_weight, down_weight, gate_mask, up_mask, down_mask):
    masked_gate = widen(gate_weight, gate_mask)
    masked_up = widen(up_weight, up_mask)
    masked_down = widen(down_weight, down_mask)
    gate = jnp.dot(tokens, masked_gate.T, preferred_element_type=jnp.float32)
    up = jnp.dot(tokens, masked_up.T, preferred_element_type=jnp.float32)
    hidden = (jax.nn.silu(gate) * up).astype(jnp.bfloat16)
    output = jnp.dot(hidden, masked_down.T, preferred_element_type=jnp.float32).astype(jnp.bfloat16)
    hidden_delta = jnp.dot(output_grad, masked_down, preferred_element_type=jnp.float32)
    sigmoid_gate = jax.nn.sigmoid(gate)
    gate_delta = (hidden_delta * up * sigmoid_gate * (1.0 + gate * (1.0 - sigmoid_gate))).astype(jnp.bfloat16)
    up_delta = (hidden_delta * jax.nn.silu(gate)).astype(jnp.bfloat16)
    down_grad = widen(jnp.dot(output_grad.T, hidden, preferred_element_type=jnp.float32), down_mask).astype(jnp.bfloat16)
    gate_grad = widen(jnp.dot(gate_delta.T, tokens, preferred_element_type=jnp.float32), gate_mask).astype(jnp.bfloat16)
    up_grad = widen(jnp.dot(up_delta.T, tokens, preferred_element_type=jnp.float32), up_mask).astype(jnp.bfloat16)
    input_grad = jnp.dot(gate_delta, masked_gate, preferred_element_type=jnp.float32)
    input_grad = (input_grad + jnp.dot(up_delta, masked_up, preferred_element_type=jnp.float32)).astype(jnp.bfloat16)
    return output, input_grad, gate_grad, up_grad, down_grad
```

```python
import functools

import jax
import jax.numpy as jnp
from jax import lax
from jax.experimental import pallas as pl
from jax.experimental.pallas import tpu as pltpu
from jax.sharding import PartitionSpec as P

B16 = jnp.bfloat16
F32 = jnp.float32
BLOCK = 128
MIB = 2**20

VMEM = pl.BlockSpec(memory_space=pltpu.VMEM)
SMEM = pl.BlockSpec(memory_space=pltpu.SMEM)
ANY = pl.BlockSpec(memory_space=pl.ANY)


def contract(left, right, left_dim, right_dim):
    return lax.dot_general(
        left, right, (((left_dim,), (right_dim,)), ((), ())), preferred_element_type=F32
    )


def keep_blocks(tile, kept):
    rows = []
    for i in range(tile.shape[0] // BLOCK):
        row = []
        for j in range(tile.shape[1] // BLOCK):
            block = tile[BLOCK * i : BLOCK * (i + 1), BLOCK * j : BLOCK * (j + 1)]
            row.append(jnp.where(kept(i, j) != 0, block, jnp.zeros_like(block)))
        rows.append(row[0] if len(row) == 1 else jnp.concatenate(row, 1))
    return rows[0] if len(rows) == 1 else jnp.concatenate(rows, 0)


def total(parts):
    return functools.reduce(lambda a, b: a + b, parts)


def fit(size, most):
    return size if size < most else most


def params(mib):
    return pltpu.CompilerParams(vmem_limit_bytes=mib * MIB)


def cost(flops, read):
    return pl.CostEstimate(flops=flops, bytes_accessed=read, transcendentals=0)


def resident(array):
    return pltpu.with_memory_space_constraint(array, pltpu.VMEM)


def down_forward(half, down_mask, grads, down, recv=None):
    tokens, depth = grads.shape
    width = down.shape[1] // 2
    tile = fit(width, 2048)
    step = fit(depth, 256)

    def kernel(half_ref, mask_ref, grads_ref, down_ref, *rest):
        out_ref = rest[-1]
        base = half_ref[0] * width

        def one(t, carry):
            start = pl.multiple_of(base + t * tile, BLOCK)
            first = start // BLOCK
            here = pl.ds(pl.multiple_of(t * tile, BLOCK), tile)
            acc = total(
                contract(
                    grads_ref[:, k : k + step],
                    keep_blocks(
                        down_ref[k : k + step, pl.ds(start, tile)],
                        lambda i, j: mask_ref[k // BLOCK + i, first + j],
                    ),
                    1,
                    0,
                )
                for k in range(0, depth, step)
            )
            if recv is not None:
                acc = acc + rest[0][:, here].astype(F32)
            out_ref[:, here] = acc.astype(B16)
            return carry

        lax.fori_loop(0, width // tile, one, 0)

    more = [] if recv is None else [recv]
    return pl.pallas_call(
        kernel,
        name="down_forward",
        in_specs=[SMEM, SMEM] + [VMEM] * (2 + len(more)),
        out_specs=VMEM,
        out_shape=jax.ShapeDtypeStruct((tokens, width), B16),
        compiler_params=params(8),
        cost_estimate=cost(8 * tokens * depth * width, 0),
    )(half, down_mask, grads, resident(down), *more)


def gate_up_forward(half, gate_mask, up_mask, tokens, gate, up, recv=None):
    count, depth = tokens.shape
    width = gate.shape[0] // 2
    tile = fit(width, 512)
    step = fit(depth, 256)

    def kernel(half_ref, gate_mask_ref, up_mask_ref, tokens_ref, gate_ref, up_ref, *rest):
        out_ref = rest[-1]
        base = half_ref[0] * width

        def one(t, carry):
            start = pl.multiple_of(base + t * tile, BLOCK)
            first = start // BLOCK
            here = pl.ds(pl.multiple_of(t * tile, BLOCK), tile)

            def product(weight_ref, mask_ref):
                return total(
                    contract(
                        keep_blocks(
                            weight_ref[pl.ds(start, tile), k : k + step],
                            lambda i, j: mask_ref[k // BLOCK + j, first + i],
                        ),
                        tokens_ref[:, k : k + step],
                        1,
                        1,
                    )
                    for k in range(0, depth, step)
                )

            both = jnp.concatenate(
                [product(gate_ref, gate_mask_ref), product(up_ref, up_mask_ref)], 1
            ).T
            if recv is not None:
                both = both + rest[0][:, here].astype(F32)
            out_ref[:, here] = both.astype(B16)
            return carry

        lax.fori_loop(0, width // tile, one, 0)

    more = [] if recv is None else [recv]
    return pl.pallas_call(
        kernel,
        name="gate_up_forward",
        in_specs=[SMEM] * 3 + [VMEM] * (3 + len(more)),
        out_specs=VMEM,
        out_shape=jax.ShapeDtypeStruct((2 * count, width), B16),
        compiler_params=params(8),
        cost_estimate=cost(16 * count * depth * width, 0),
    )(half, gate_mask.T, up_mask.T, tokens, resident(gate), resident(up), *more)


def local_deltas(delta, delta_far, pre, pre_far):
    count, width = delta.shape

    def kernel(delta_ref, delta_far_ref, pre_ref, pre_far_ref, out_ref):
        hidden_delta = delta_ref[...].astype(F32) + delta_far_ref[...].astype(F32)
        both = pre_ref[...].astype(F32) + pre_far_ref[...].astype(F32)
        gate, up = both[:count], both[count:]
        sigmoid = jax.nn.sigmoid(gate)
        silu = gate * sigmoid
        out_ref[:count] = (silu * up).astype(B16)
        out_ref[count : 2 * count] = (
            hidden_delta * up * sigmoid * (1.0 + gate * (1.0 - sigmoid))
        ).astype(B16)
        out_ref[2 * count :] = (hidden_delta * silu).astype(B16)

    return pl.pallas_call(
        kernel,
        name="local_deltas",
        in_specs=[VMEM] * 4,
        out_specs=VMEM,
        out_shape=jax.ShapeDtypeStruct((3 * count, width), B16),
        compiler_params=params(8),
        cost_estimate=cost(count * width * 100, 0),
    )(delta, delta_far, pre, pre_far)


def backward(half, masks, weights, acts, before, blocks):
    gate, up, down = weights
    count = acts.shape[0] // 3
    width = acts.shape[1]
    depth = gate.shape[1]
    tile = fit(depth // 2, 512)
    step = fit(width, 256)
    rows = count // blocks

    def kernel(half_ref, gate_mask_ref, up_mask_ref, down_mask_ref, gate_ref, up_ref, down_ref, acts_ref, *rest):
        base = half_ref[0] * width

        def one(t, carry):
            spans = [pl.multiple_of((2 * t + n) * tile, BLOCK) for n in range(2)]
            outs, ins = [], []
            for span in spans:
                first = span // BLOCK
                outs.append(
                    total(
                        contract(
                            keep_blocks(
                                down_ref[pl.ds(span, tile), pl.ds(pl.multiple_of(base + k, BLOCK), step)],
                                lambda i, j: down_mask_ref[first + i, (base + k) // BLOCK + j],
                            ),
                            acts_ref[:count, k : k + step],
                            1,
                            1,
                        )
                        for k in range(0, width, step)
                    )
                )
            both = jnp.concatenate(outs, 1).T
            for n, span in enumerate(spans):
                first = span // BLOCK
                parts = []
                for weight_ref, mask_ref, row in (
                    (gate_ref, gate_mask_ref, count),
                    (up_ref, up_mask_ref, 2 * count),
                ):
                    for k in range(0, width, step):
                        parts.append(
                            contract(
                                acts_ref[row : row + count, k : k + step],
                                keep_blocks(
                                    weight_ref[pl.ds(pl.multiple_of(base + k, BLOCK), step), pl.ds(span, tile)],
                                    lambda i, j: mask_ref[first + j, (base + k) // BLOCK + i],
                                ),
                                1,
                                0,
                            )
                        )
                ins = total(parts)
                out = both[n * count : (n + 1) * count]
                here = pl.ds(span, tile)
                if before is None:
                    rest[0][:count, here] = out
                    rest[0][count:, here] = ins
                else:
                    out = (out + rest[0][:count, here]).astype(B16)
                    ins = (ins + rest[0][count:, here]).astype(B16)
                    for b in range(blocks):
                        rest[1 + b][:rows, here] = out[b * rows : (b + 1) * rows]
                        rest[1 + b][rows:, here] = ins[b * rows : (b + 1) * rows]
            return carry

        lax.fori_loop(0, depth // (2 * tile), one, 0)

    if before is None:
        more, out_shape = [], [jax.ShapeDtypeStruct((2 * count, depth), F32)]
    else:
        more, out_shape = [before], [jax.ShapeDtypeStruct((2 * rows, depth), B16)] * blocks
    return pl.pallas_call(
        kernel,
        name="backward",
        in_specs=[SMEM] * 4 + [VMEM] * (4 + len(more)),
        out_specs=[VMEM] * len(out_shape),
        out_shape=out_shape,
        compiler_params=params(8),
        cost_estimate=cost(24 * count * depth * width, 0),
    )(half, masks[0].T, masks[1].T, masks[2], *[resident(w) for w in weights], acts, *more)


def weight_grads(halves, masks, tokens, grads, acts):
    count, depth = tokens.shape
    width = acts[0].shape[1]
    tall = fit(width, 1024)
    wide = fit(depth, 512)
    tall_d = fit(depth, 1024)
    wide_h = fit(width, 512)
    slots = 4

    def kernel(halves_ref, gate_mask_ref, up_mask_ref, down_mask_ref, tokens_ref, grads_ref, own_ref, far_ref,
               gate_out, up_out, down_out, ring, sems):
        pending = [None] * slots
        turn = 0

        def emit(tile, target):
            nonlocal turn
            slot = turn % slots
            turn += 1
            if pending[slot] is not None:
                pending[slot].wait()
            space = ring.at[slot, : tile.shape[0], : tile.shape[1]]
            space[...] = tile
            pending[slot] = pltpu.make_async_copy(space, target, sems.at[slot])
            pending[slot].start()

        for n, acts_ref in enumerate((own_ref, far_ref)):
            base = halves_ref[n] * width
            for out_ref, mask_ref, row in ((gate_out, gate_mask_ref, count), (up_out, up_mask_ref, 2 * count)):
                for h in range(0, width, tall):
                    for d in range(0, depth, wide):
                        start = pl.multiple_of(base + h, BLOCK)
                        tile = contract(
                            acts_ref[row : row + count, h : h + tall], tokens_ref[:, d : d + wide], 0, 0
                        ).astype(B16)
                        tile = keep_blocks(
                            tile, lambda i, j: mask_ref[d // BLOCK + j, start // BLOCK + i]
                        )
                        emit(tile, out_ref.at[pl.ds(start, tall), pl.ds(d, wide)])
            for h in range(0, width, wide_h):
                for d in range(0, depth, tall_d):
                    start = pl.multiple_of(base + h, BLOCK)
                    tile = contract(
                        grads_ref[:, d : d + tall_d], acts_ref[:count, h : h + wide_h], 0, 0
                    ).astype(B16)
                    tile = keep_blocks(
                        tile, lambda i, j: down_mask_ref[d // BLOCK + i, start // BLOCK + j]
                    )
                    emit(tile, down_out.at[pl.ds(d, tall_d), pl.ds(start, wide_h)])
        for copy in pending:
            if copy is not None:
                copy.wait()

    return pl.pallas_call(
        kernel,
        name="weight_grads",
        in_specs=[SMEM] * 4 + [VMEM] * 4,
        out_specs=[ANY] * 3,
        out_shape=[
            jax.ShapeDtypeStruct((2 * width, depth), B16),
            jax.ShapeDtypeStruct((2 * width, depth), B16),
            jax.ShapeDtypeStruct((depth, 2 * width), B16),
        ],
        scratch_shapes=[
            pltpu.VMEM((slots, max(tall, tall_d), max(wide, wide_h)), B16),
            pltpu.SemaphoreType.DMA((slots,)),
        ],
        compiler_params=params(16),
        cost_estimate=cost(0, 12 * width * depth),
    )(halves, masks[0].T, masks[1].T, masks[2], tokens, grads, *acts)


def body(rows, tokens, output_grad, gate_weight, up_weight, down_weight, gate_mask, up_mask, down_mask):
    masks = (gate_mask, up_mask, down_mask)
    weights = (gate_weight, up_weight, down_weight)
    direct = rows <= 4

    def gather(array):
        if not direct:
            return lax.all_gather(array, "row", axis=0, tiled=True)
        parts = [array]
        for s in range(1, rows):
            parts.append(lax.ppermute(array, "row", [(i, (i + s) % rows) for i in range(rows)]))
        return jnp.concatenate(parts, 0)

    def swap(array, bit):
        size = lax.axis_size("col")
        return lax.ppermute(array, "col", [(i, i ^ bit) for i in range(size)])

    mine = lax.axis_index("col") % 2
    own = jnp.reshape(mine, (1,)).astype(jnp.int32)
    far = 1 - own

    all_grads = gather(output_grad)
    all_tokens = gather(tokens)

    delta_sent = swap(down_forward(far, down_mask, all_grads, down_weight), 1)
    pre_sent = swap(gate_up_forward(far, gate_mask, up_mask, all_tokens, gate_weight, up_weight), 1)
    delta = down_forward(own, down_mask, all_grads, down_weight, delta_sent)
    delta_far = swap(delta, 2)
    pre = gate_up_forward(own, gate_mask, up_mask, all_tokens, gate_weight, up_weight, pre_sent)
    pre_far = swap(pre, 2)
    acts = local_deltas(delta, delta_far, pre, pre_far)
    acts_far = swap(acts, 1)

    first = backward(own, masks, weights, acts, None, 1)
    blocks = backward(far, masks, weights, acts_far, first[0], rows if direct else 1)
    count = tokens.shape[0]
    if direct:
        pieces = [blocks[0]]
        for s in range(1, rows):
            pieces.append(lax.ppermute(blocks[s], "row", [(i, (i - s) % rows) for i in range(rows)]))
        summed = total(p.astype(F32) for p in pieces).astype(B16)
        output, input_grad = summed[:count], summed[count:]
    else:
        half = blocks[0].shape[0] // 2
        output, input_grad = [
            lax.psum_scatter(part, "row", scatter_dimension=0, tiled=True)
            for part in (blocks[0][:half], blocks[0][half:])
        ]
    gate_grad, up_grad, down_grad = weight_grads(
        jnp.concatenate([own, far]), masks, all_tokens, all_grads, (acts, acts_far)
    )
    return output, input_grad, gate_grad, up_grad, down_grad


def solution(mesh):
    rows = mesh.shape["row"]
    held = P(("member", "row"), "col")
    return jax.shard_map(
        functools.partial(body, rows),
        mesh=mesh,
        in_specs=(held, held, held, held, P(("member", "col"), "row"), P("row", "col"), P("row", "col"), P("col", "row")),
        out_specs=(held, held, held, held, P(("member", "col"), "row")),
        check_vma=False,
    )
```

```python
import functools

import jax
import jax.numpy as jnp
from jax import lax
from jax.experimental import pallas as pl
from jax.experimental.pallas import tpu as pltpu
from jax.sharding import PartitionSpec as P

B16 = jnp.bfloat16
F32 = jnp.float32
BLOCK = 128
MIB = 2**20
OWN, FAR = 0, 1

VMEM = pl.BlockSpec(memory_space=pltpu.VMEM)
SMEM = pl.BlockSpec(memory_space=pltpu.SMEM)
ANY = pl.BlockSpec(memory_space=pl.ANY)


def contract(left, right, left_dim, right_dim):
    return lax.dot_general(
        left, right, (((left_dim,), (right_dim,)), ((), ())), preferred_element_type=F32
    )


def keep_blocks(tile, kept):
    rows = []
    for i in range(tile.shape[0] // BLOCK):
        row = []
        for j in range(tile.shape[1] // BLOCK):
            block = tile[BLOCK * i : BLOCK * (i + 1), BLOCK * j : BLOCK * (j + 1)]
            row.append(jnp.where(kept(i, j) != 0, block, jnp.zeros_like(block)))
        rows.append(row[0] if len(row) == 1 else jnp.concatenate(row, 1))
    return rows[0] if len(rows) == 1 else jnp.concatenate(rows, 0)


def stacked(refs, span):
    parts = [ref[:, span] for ref in refs]
    return parts[0] if len(parts) == 1 else jnp.concatenate(parts, 0)


def half_of_pair(side):
    return (lax.axis_index("col") + side) % 2


def total(parts):
    return functools.reduce(lambda a, b: a + b, parts)


def fit(size, most):
    return size if size < most else most


def params(mib):
    return pltpu.CompilerParams(vmem_limit_bytes=mib * MIB)


def cost(flops, read):
    return pl.CostEstimate(flops=flops, bytes_accessed=read, transcendentals=0)


def resident(arrays):
    return [pltpu.with_memory_space_constraint(a, pltpu.VMEM) for a in arrays]


def load(weights, hidden_dims, pieces):
    count = len(weights)
    shapes = []
    for weight, dim in zip(weights, hidden_dims):
        shape = list(weight.shape)
        shape[dim] //= 2 * pieces
        shapes += [tuple(shape)] * (2 * pieces)

    def kernel(*refs):
        outs, sems = refs[count:-1], refs[-1]
        copies = []
        for n, dim in enumerate(hidden_dims):
            for side in (OWN, FAR):
                for p in range(pieces):
                    at = len(copies)
                    size = shapes[at][dim]
                    span = pl.ds(
                        pl.multiple_of((half_of_pair(side) * pieces + p) * size, BLOCK), size
                    )
                    source = refs[n].at[span] if dim == 0 else refs[n].at[:, span]
                    copies.append(pltpu.make_async_copy(source, outs[at], sems.at[at]))
        for copy in copies:
            copy.start()
        for copy in copies:
            copy.wait()

    loaded = pl.pallas_call(
        kernel,
        name="load",
        in_specs=[ANY] * count,
        out_specs=[VMEM] * len(shapes),
        out_shape=[pltpu.VMEM(s, B16) for s in shapes],
        scratch_shapes=[pltpu.SemaphoreType.DMA((len(shapes),))],
        compiler_params=params(1),
        cost_estimate=cost(0, sum(w.size * 2 for w in weights)),
    )(*[pltpu.with_memory_space_constraint(w, pltpu.HBM) for w in weights])
    return [
        [loaded[(2 * n + side) * pieces : (2 * n + side + 1) * pieces] for side in (OWN, FAR)]
        for n in range(count)
    ]


def down_forward(side, mask, weight, grads, recv=None):
    pieces, parts = len(weight), len(grads)
    tokens, depth = parts * grads[0].shape[0], grads[0].shape[1]
    width = weight[0].shape[1]
    tile = fit(width, 1024)
    step = fit(depth, 256)

    def kernel(mask_ref, *rest):
        weight_refs, grads_refs = rest[:pieces], rest[pieces : pieces + parts]
        out_ref = rest[-1]
        for p in range(pieces):
            base = (half_of_pair(side) * pieces + p) * (width // BLOCK)

            def one(t, carry):
                start = pl.multiple_of(t * tile, BLOCK)
                here = pl.ds(pl.multiple_of(p * width + t * tile, BLOCK), tile)
                acc = total(
                    contract(
                        stacked(grads_refs, slice(k, k + step)),
                        keep_blocks(
                            weight_refs[p][k : k + step, pl.ds(start, tile)],
                            lambda i, j: mask_ref[k // BLOCK + i, base + start // BLOCK + j],
                        ),
                        1,
                        0,
                    )
                    for k in range(0, depth, step)
                )
                if recv is not None:
                    acc = acc + rest[-2][:, here].astype(F32)
                out_ref[:, here] = acc.astype(B16)
                return carry

            lax.fori_loop(0, width // tile, one, 0)

    more = [] if recv is None else [recv]
    return pl.pallas_call(
        kernel,
        name="down_forward",
        in_specs=[SMEM] + [VMEM] * (pieces + parts + len(more)),
        out_specs=VMEM,
        out_shape=jax.ShapeDtypeStruct((tokens, pieces * width), B16),
        compiler_params=params(6),
        cost_estimate=cost(8 * tokens * depth * width * pieces, 0),
    )(mask, *resident(weight), *grads, *more)


def up_forward(side, mask, weight, tokens, recv=None):
    pieces, parts = len(weight), len(tokens)
    count, depth = parts * tokens[0].shape[0], tokens[0].shape[1]
    width = weight[0].shape[0]
    tile = fit(width // 2, 512)
    step = fit(depth, 256)

    def kernel(mask_ref, *rest):
        weight_refs, tokens_refs = rest[:pieces], rest[pieces : pieces + parts]
        out_ref = rest[-1]
        for p in range(pieces):
            base = (half_of_pair(side) * pieces + p) * (width // BLOCK)

            def one(t, carry):
                starts = [pl.multiple_of((2 * t + n) * tile, BLOCK) for n in range(2)]
                both = jnp.concatenate(
                    [
                        total(
                            contract(
                                keep_blocks(
                                    weight_refs[p][pl.ds(start, tile), k : k + step],
                                    lambda i, j: mask_ref[k // BLOCK + j, base + start // BLOCK + i],
                                ),
                                stacked(tokens_refs, slice(k, k + step)),
                                1,
                                1,
                            )
                            for k in range(0, depth, step)
                        )
                        for start in starts
                    ],
                    1,
                ).T
                for n in range(2):
                    here = pl.ds(pl.multiple_of(p * width + (2 * t + n) * tile, BLOCK), tile)
                    out = both[n * count : (n + 1) * count]
                    if recv is not None:
                        out = out + rest[-2][:, here].astype(F32)
                    out_ref[:, here] = out.astype(B16)
                return carry

            lax.fori_loop(0, width // (2 * tile), one, 0)

    more = [] if recv is None else [recv]
    return pl.pallas_call(
        kernel,
        name="up_forward",
        in_specs=[SMEM] + [VMEM] * (pieces + parts + len(more)),
        out_specs=VMEM,
        out_shape=jax.ShapeDtypeStruct((count, pieces * width), B16),
        compiler_params=params(6),
        cost_estimate=cost(8 * count * depth * width * pieces, 0),
    )(mask.T, *resident(weight), *tokens, *more)


def activate(gate, gate_far, up, up_far):
    def kernel(gate_ref, gate_far_ref, up_ref, up_far_ref, out_ref):
        gate_sum = gate_ref[...].astype(F32) + gate_far_ref[...].astype(F32)
        up_sum = up_ref[...].astype(F32) + up_far_ref[...].astype(F32)
        out_ref[...] = (gate_sum * jax.nn.sigmoid(gate_sum) * up_sum).astype(B16)

    return pl.pallas_call(
        kernel,
        name="activate",
        in_specs=[VMEM] * 4,
        out_specs=VMEM,
        out_shape=jax.ShapeDtypeStruct(gate.shape, B16),
        compiler_params=params(6),
        cost_estimate=cost(gate.size * 300, 0),
    )(gate, gate_far, up, up_far)


def deltas(gate, gate_far, up, up_far, delta, delta_far):
    count, width = gate.shape

    def kernel(gate_ref, gate_far_ref, up_ref, up_far_ref, delta_ref, delta_far_ref, out_ref):
        gate_sum = gate_ref[...].astype(F32) + gate_far_ref[...].astype(F32)
        up_sum = up_ref[...].astype(F32) + up_far_ref[...].astype(F32)
        hidden_delta = delta_ref[...].astype(F32) + delta_far_ref[...].astype(F32)
        sigmoid = jax.nn.sigmoid(gate_sum)
        out_ref[:count] = (
            hidden_delta * up_sum * sigmoid * (1.0 + gate_sum * (1.0 - sigmoid))
        ).astype(B16)
        out_ref[count:] = (hidden_delta * (gate_sum * sigmoid)).astype(B16)

    return pl.pallas_call(
        kernel,
        name="deltas",
        in_specs=[VMEM] * 6,
        out_specs=VMEM,
        out_shape=jax.ShapeDtypeStruct((2 * count, width), B16),
        compiler_params=params(6),
        cost_estimate=cost(gate.size * 300, 0),
    )(gate, gate_far, up, up_far, delta, delta_far)


def output_part(side, mask, weight, hidden, before=None):
    pieces = len(weight)
    count = hidden.shape[0]
    depth, width = weight[0].shape
    tile = fit(depth // 2, 512)
    step = fit(width, 256)

    def kernel(mask_ref, *rest):
        weight_refs, hidden_ref, out_ref = rest[:pieces], rest[pieces], rest[-1]
        base = half_of_pair(side) * pieces * (width // BLOCK)

        def one(t, carry):
            starts = [pl.multiple_of((2 * t + n) * tile, BLOCK) for n in range(2)]
            both = jnp.concatenate(
                [
                    total(
                        contract(
                            keep_blocks(
                                weight_refs[p][pl.ds(start, tile), k : k + step],
                                lambda i, j: mask_ref[
                                    start // BLOCK + i, base + (p * width + k) // BLOCK + j
                                ],
                            ),
                            hidden_ref[:, p * width + k : p * width + k + step],
                            1,
                            1,
                        )
                        for p in range(pieces)
                        for k in range(0, width, step)
                    )
                    for start in starts
                ],
                1,
            ).T
            for n, start in enumerate(starts):
                out = both[n * count : (n + 1) * count]
                if before is not None:
                    out = out + rest[-2][:, pl.ds(start, tile)]
                out_ref[:, pl.ds(start, tile)] = out
            return carry

        lax.fori_loop(0, depth // (2 * tile), one, 0)

    more = [] if before is None else [before]
    return pl.pallas_call(
        kernel,
        name="output_part",
        in_specs=[SMEM] + [VMEM] * (pieces + 1 + len(more)),
        out_specs=VMEM,
        out_shape=jax.ShapeDtypeStruct((count, depth), F32),
        compiler_params=params(6),
        cost_estimate=cost(8 * count * depth * width * pieces, 0),
    )(mask, *resident(weight), hidden, *more)


def input_part(side, masks, gate, up, delta, before=None, output=None, blocks=1):
    pieces = len(gate)
    count = delta.shape[0] // 2
    width, depth = gate[0].shape
    tile = fit(depth, 1024)
    step = fit(width, 256)
    rows = count // blocks

    def kernel(gate_mask_ref, up_mask_ref, *rest):
        gate_refs, up_refs, delta_ref = rest[:pieces], rest[pieces : 2 * pieces], rest[2 * pieces]
        rest = rest[2 * pieces + 1 :]
        base = half_of_pair(side) * pieces * (width // BLOCK)

        def one(t, carry):
            start = pl.multiple_of(t * tile, BLOCK)
            here = pl.ds(start, tile)
            acc = total(
                contract(
                    delta_ref[row : row + count, p * width + k : p * width + k + step],
                    keep_blocks(
                        refs[p][k : k + step, here],
                        lambda i, j: mask_ref[
                            start // BLOCK + j, base + (p * width + k) // BLOCK + i
                        ],
                    ),
                    1,
                    0,
                )
                for refs, mask_ref, row in (
                    (gate_refs, gate_mask_ref, 0),
                    (up_refs, up_mask_ref, count),
                )
                for p in range(pieces)
                for k in range(0, width, step)
            )
            if before is None:
                rest[0][:, here] = acc
            else:
                acc = (acc + rest[0][:, here]).astype(B16)
                out = rest[1][:, here].astype(B16)
                for b in range(blocks):
                    rest[2 + b][:rows, here] = out[b * rows : (b + 1) * rows]
                    rest[2 + b][rows:, here] = acc[b * rows : (b + 1) * rows]
            return carry

        lax.fori_loop(0, depth // tile, one, 0)

    if before is None:
        more, out_shape = [], [jax.ShapeDtypeStruct((count, depth), F32)]
    else:
        more = [before, output]
        out_shape = [jax.ShapeDtypeStruct((2 * rows, depth), B16)] * blocks
    return pl.pallas_call(
        kernel,
        name="input_part",
        in_specs=[SMEM] * 2 + [VMEM] * (2 * pieces + 1 + len(more)),
        out_specs=[VMEM] * len(out_shape),
        out_shape=out_shape,
        compiler_params=params(6),
        cost_estimate=cost(16 * count * depth * width * pieces, 0),
    )(masks[0].T, masks[1].T, *resident(gate), *resident(up), delta, *more)


def weight_grads(masks, tokens, grads, hidden, delta):
    parts = len(tokens)
    count, depth = parts * tokens[0].shape[0], tokens[0].shape[1]
    width = hidden[0].shape[1]
    tall = fit(width, 1024)
    wide = fit(depth, 512)
    tall_d = fit(depth, 1024)
    wide_h = fit(width, 512)
    slots = 4

    def kernel(gate_mask_ref, up_mask_ref, down_mask_ref, *rest):
        hidden_refs, delta_refs = rest[:2], rest[2:4]
        rest = rest[4:]
        tokens_refs, grads_refs = rest[:parts], rest[parts : 2 * parts]
        gate_out, up_out, down_out, ring, sems = rest[2 * parts :]
        pending = [None] * slots
        turn = 0

        def emit(tile, target):
            nonlocal turn
            slot = turn % slots
            turn += 1
            if pending[slot] is not None:
                pending[slot].wait()
            space = ring.at[slot, : tile.shape[0], : tile.shape[1]]
            space[...] = tile
            pending[slot] = pltpu.make_async_copy(space, target, sems.at[slot])
            pending[slot].start()

        for side in (OWN, FAR):
            base = half_of_pair(side) * width
            for h in range(0, width, wide_h):
                for d in range(0, depth, tall_d):
                    start = pl.multiple_of(base + h, BLOCK)
                    tile = contract(
                        stacked(grads_refs, slice(d, d + tall_d)),
                        hidden_refs[side][:, h : h + wide_h],
                        0,
                        0,
                    ).astype(B16)
                    tile = keep_blocks(
                        tile, lambda i, j: down_mask_ref[d // BLOCK + i, start // BLOCK + j]
                    )
                    emit(tile, down_out.at[pl.ds(d, tall_d), pl.ds(start, wide_h)])
            for out_ref, mask_ref, row in (
                (gate_out, gate_mask_ref, 0),
                (up_out, up_mask_ref, count),
            ):
                for h in range(0, width, tall):
                    for d in range(0, depth, wide):
                        start = pl.multiple_of(base + h, BLOCK)
                        tile = contract(
                            delta_refs[side][row : row + count, h : h + tall],
                            stacked(tokens_refs, slice(d, d + wide)),
                            0,
                            0,
                        ).astype(B16)
                        tile = keep_blocks(
                            tile, lambda i, j: mask_ref[d // BLOCK + j, start // BLOCK + i]
                        )
                        emit(tile, out_ref.at[pl.ds(start, tall), pl.ds(d, wide)])
        for copy in pending:
            if copy is not None:
                copy.wait()

    return pl.pallas_call(
        kernel,
        name="weight_grads",
        in_specs=[SMEM] * 3 + [VMEM] * (4 + 2 * parts),
        out_specs=[ANY] * 3,
        out_shape=[
            jax.ShapeDtypeStruct((2 * width, depth), B16),
            jax.ShapeDtypeStruct((2 * width, depth), B16),
            jax.ShapeDtypeStruct((depth, 2 * width), B16),
        ],
        scratch_shapes=[
            pltpu.VMEM((slots, max(tall, tall_d), max(wide, wide_h)), B16),
            pltpu.SemaphoreType.DMA((slots,)),
        ],
        compiler_params=params(16),
        cost_estimate=cost(0, 12 * width * depth),
    )(masks[0].T, masks[1].T, masks[2], *hidden, *delta, *tokens, *grads)


def body(rows, tokens, output_grad, gate_weight, up_weight, down_weight, gate_mask, up_mask, down_mask):
    masks = (gate_mask, up_mask, down_mask)
    direct = rows <= 4
    pieces = 2 if gate_weight.shape[0] >= 2048 else 1

    def gather(array):
        if not direct:
            return [lax.all_gather(array, "row", axis=0, tiled=True)]
        return [array] + [
            lax.ppermute(array, "row", [(i, (i + s) % rows) for i in range(rows)])
            for s in range(1, rows)
        ]

    def swap(array, bit):
        size = lax.axis_size("col")
        return lax.ppermute(array, "col", [(i, i ^ bit) for i in range(size)])

    all_tokens = gather(tokens)
    all_grads = gather(output_grad)
    gate_w, up_w, down_w = load((gate_weight, up_weight, down_weight), (0, 0, 1), pieces)

    sent = swap(up_forward(FAR, gate_mask, gate_w[FAR], all_tokens), 1)
    gate = up_forward(OWN, gate_mask, gate_w[OWN], all_tokens, sent)
    gate_far = swap(gate, 2)
    sent = swap(up_forward(FAR, up_mask, up_w[FAR], all_tokens), 1)
    up = up_forward(OWN, up_mask, up_w[OWN], all_tokens, sent)
    up_far = swap(up, 2)
    sent = swap(down_forward(FAR, down_mask, down_w[FAR], all_grads), 1)
    delta = down_forward(OWN, down_mask, down_w[OWN], all_grads, sent)
    delta_far = swap(delta, 2)

    hidden = activate(gate, gate_far, up, up_far)
    hidden = (hidden, swap(hidden, 1))
    out = output_part(OWN, down_mask, down_w[OWN], hidden[OWN])
    out = output_part(FAR, down_mask, down_w[FAR], hidden[FAR], out)
    both = deltas(gate, gate_far, up, up_far, delta, delta_far)
    both = (both, swap(both, 1))
    first = input_part(OWN, masks, gate_w[OWN], up_w[OWN], both[OWN])
    blocks = input_part(
        FAR, masks, gate_w[FAR], up_w[FAR], both[FAR], first[0], out, rows if direct else 1
    )
    count = tokens.shape[0]
    if direct:
        parts = [blocks[0]]
        for s in range(1, rows):
            parts.append(lax.ppermute(blocks[s], "row", [(i, (i - s) % rows) for i in range(rows)]))
        summed = total(p.astype(F32) for p in parts).astype(B16)
        output, input_grad = summed[:count], summed[count:]
    else:
        half = blocks[0].shape[0] // 2
        output, input_grad = [
            lax.psum_scatter(part, "row", scatter_dimension=0, tiled=True)
            for part in (blocks[0][:half], blocks[0][half:])
        ]
    gate_grad, up_grad, down_grad = weight_grads(masks, all_tokens, all_grads, hidden, both)
    return output, input_grad, gate_grad, up_grad, down_grad


def solution(mesh):
    rows = mesh.shape["row"]
    held = P(("member", "row"), "col")
    down_held = P(("member", "col"), "row")
    return jax.shard_map(
        functools.partial(body, rows),
        mesh=mesh,
        in_specs=(held, held, held, held, down_held, P("row", "col"), P("row", "col"), P("col", "row")),
        out_specs=(held, held, held, held, down_held),
        check_vma=False,
    )
```

```python
import functools

import jax
import jax.numpy as jnp
from jax import lax
from jax.experimental import pallas as pl
from jax.experimental.pallas import tpu as pltpu
from jax.sharding import PartitionSpec as P

B16 = jnp.bfloat16
F32 = jnp.float32
BLOCK = 128
MIB = 2**20
OWN, FAR = 0, 1
CUTS = 1

VMEM = pl.BlockSpec(memory_space=pltpu.VMEM)
SMEM = pl.BlockSpec(memory_space=pltpu.SMEM)
ANY = pl.BlockSpec(memory_space=pl.ANY)


def contract(left, right, left_dim, right_dim):
    return lax.dot_general(
        left, right, (((left_dim,), (right_dim,)), ((), ())), preferred_element_type=F32
    )


def keep_blocks(tile, kept):
    rows = []
    for i in range(tile.shape[0] // BLOCK):
        row = []
        for j in range(tile.shape[1] // BLOCK):
            block = tile[BLOCK * i : BLOCK * (i + 1), BLOCK * j : BLOCK * (j + 1)]
            row.append(jnp.where(kept(i, j) != 0, block, jnp.zeros_like(block)))
        rows.append(row[0] if len(row) == 1 else jnp.concatenate(row, 1))
    return rows[0] if len(rows) == 1 else jnp.concatenate(rows, 0)


def stacked(refs, rows, span):
    parts = [ref[rows, span] for ref in refs]
    return parts[0] if len(parts) == 1 else jnp.concatenate(parts, 0)


def half_of_pair(side):
    return (lax.axis_index("col") + side) % 2


def total(parts):
    return functools.reduce(lambda a, b: a + b, parts)


def fit(size, most):
    return size if size < most else most


def params(mib):
    return pltpu.CompilerParams(vmem_limit_bytes=mib * MIB)


def cost(flops, read):
    return pl.CostEstimate(flops=flops, bytes_accessed=read, transcendentals=0)


def resident(arrays):
    return [pltpu.with_memory_space_constraint(a, pltpu.VMEM) for a in arrays]


def piece_shapes(weight, dim, pieces):
    shape = list(weight.shape)
    shape[dim] //= 2 * pieces
    return [tuple(shape)] * pieces


def piece_copies(source_ref, dim, side, out_refs, sems):
    copies = []
    for p, out_ref in enumerate(out_refs):
        height, size = out_ref.shape[0] // CUTS, out_ref.shape[dim]
        first = pl.multiple_of((half_of_pair(side) * len(out_refs) + p) * size, BLOCK)
        for cut in range(CUTS):
            here = pl.ds(cut * height, height)
            if dim == 0:
                source = source_ref.at[pl.ds(first + cut * height, height)]
            else:
                source = source_ref.at[here, pl.ds(first, size)]
            copies.append(
                pltpu.make_async_copy(source, out_ref.at[here], sems.at[p * CUTS + cut])
            )
    return copies


def join(top, bottom):
    height, width = top.shape

    def kernel(top_ref, bottom_ref, out_ref, sems):
        copies = [
            pltpu.make_async_copy(ref, out_ref.at[pl.ds(n * height, height)], sems.at[n])
            for n, ref in enumerate((top_ref, bottom_ref))
        ]
        for copy in copies:
            copy.start()
        for copy in copies:
            copy.wait()

    return pl.pallas_call(
        kernel,
        name="join",
        in_specs=[ANY] * 2,
        out_specs=VMEM,
        out_shape=jax.ShapeDtypeStruct((2 * height, width), top.dtype),
        scratch_shapes=[pltpu.SemaphoreType.DMA((2,))],
        compiler_params=params(1),
    )(in_hbm(top), in_hbm(bottom))


def in_hbm(array):
    return pltpu.with_memory_space_constraint(array, pltpu.HBM)


def load(items, pieces):
    count = len(items)
    shapes = [s for weight, dim in items for s in piece_shapes(weight, dim, pieces) * 2]

    def kernel(*refs):
        outs, sems = refs[count:-1], refs[-1]
        copies = []
        for n, (_, dim) in enumerate(items):
            for side in (OWN, FAR):
                at = (2 * n + side) * pieces
                copies += piece_copies(
                    refs[n], dim, side, outs[at : at + pieces],
                    sems.at[pl.ds(at * CUTS, pieces * CUTS)],
                )
        for copy in copies:
            copy.start()
        for copy in copies:
            copy.wait()

    loaded = pl.pallas_call(
        kernel,
        name="load",
        in_specs=[ANY] * count,
        out_specs=[VMEM] * len(shapes),
        out_shape=[pltpu.VMEM(s, B16) for s in shapes],
        scratch_shapes=[pltpu.SemaphoreType.DMA((len(shapes) * CUTS,))],
        compiler_params=params(1),
        cost_estimate=cost(0, sum(w.size * 2 for w, _ in items)),
    )(*[in_hbm(w) for w, _ in items])
    return [
        [loaded[(2 * n + side) * pieces : (2 * n + side + 1) * pieces] for side in (OWN, FAR)]
        for n in range(count)
    ]


def down_forward(side, mask, weight, grads, recv=None, after=()):
    pieces, parts = len(weight), len(grads)
    rows, depth = grads[0].shape[0] // 2, grads[0].shape[1]
    tokens = parts * rows
    width = weight[0].shape[1]
    tile = fit(width, 1024)
    step = fit(depth, 256)

    def kernel(mask_ref, *rest):
        weight_refs, grads_refs = rest[:pieces], rest[pieces : pieces + parts]
        recv_ref, out_ref = rest[pieces + parts], rest[-1]
        for p in range(pieces):
            base = (half_of_pair(side) * pieces + p) * (width // BLOCK)

            def one(t, carry):
                start = pl.multiple_of(t * tile, BLOCK)
                here = pl.ds(pl.multiple_of(p * width + t * tile, BLOCK), tile)
                acc = total(
                    contract(
                        stacked(grads_refs, slice(rows, None), slice(k, k + step)),
                        keep_blocks(
                            weight_refs[p][k : k + step, pl.ds(start, tile)],
                            lambda i, j: mask_ref[k // BLOCK + i, base + start // BLOCK + j],
                        ),
                        1,
                        0,
                    )
                    for k in range(0, depth, step)
                )
                if recv is not None:
                    acc = acc + recv_ref[:, here].astype(F32)
                out_ref[:, here] = acc.astype(B16)
                return carry

            lax.fori_loop(0, width // tile, one, 0)

    more = [] if recv is None else [recv]
    return pl.pallas_call(
        kernel,
        name="down_forward",
        in_specs=[SMEM] + [VMEM] * (pieces + parts + len(more)) + [ANY] * len(after),
        out_specs=VMEM,
        out_shape=jax.ShapeDtypeStruct((tokens, pieces * width), B16),
        compiler_params=params(4),
        cost_estimate=cost(1, 1),
    )(mask, *resident(weight), *grads, *more, *after)


def up_forward(side, mask, weight, tokens, recv=None, after=()):
    pieces, parts = len(weight), len(tokens)
    rows, depth = tokens[0].shape[0] // 2, tokens[0].shape[1]
    count = parts * rows
    width = weight[0].shape[0]
    tile = fit(width // 2, 512)
    step = fit(depth, 256)

    def kernel(mask_ref, *rest):
        weight_refs, tokens_refs = rest[:pieces], rest[pieces : pieces + parts]
        recv_ref, out_ref = rest[pieces + parts], rest[-1]
        for p in range(pieces):
            base = (half_of_pair(side) * pieces + p) * (width // BLOCK)

            def one(t, carry):
                starts = [pl.multiple_of((2 * t + n) * tile, BLOCK) for n in range(2)]
                both = jnp.concatenate(
                    [
                        total(
                            contract(
                                keep_blocks(
                                    weight_refs[p][pl.ds(start, tile), k : k + step],
                                    lambda i, j: mask_ref[k // BLOCK + j, base + start // BLOCK + i],
                                ),
                                stacked(tokens_refs, slice(0, rows), slice(k, k + step)),
                                1,
                                1,
                            )
                            for k in range(0, depth, step)
                        )
                        for start in starts
                    ],
                    1,
                ).T
                for n in range(2):
                    here = pl.ds(pl.multiple_of(p * width + (2 * t + n) * tile, BLOCK), tile)
                    out = both[n * count : (n + 1) * count]
                    if recv is not None:
                        out = out + recv_ref[:, here].astype(F32)
                    out_ref[:, here] = out.astype(B16)
                return carry

            lax.fori_loop(0, width // (2 * tile), one, 0)

    more = [] if recv is None else [recv]
    return pl.pallas_call(
        kernel,
        name="up_forward",
        in_specs=[SMEM] + [VMEM] * (pieces + parts + len(more)) + [ANY] * len(after),
        out_specs=VMEM,
        out_shape=jax.ShapeDtypeStruct((count, pieces * width), B16),
        compiler_params=params(4),
        cost_estimate=cost(1, 1),
    )(mask.T, *resident(weight), *tokens, *more, *after)


def activate(gate, gate_far, up, up_far):
    def kernel(gate_ref, gate_far_ref, up_ref, up_far_ref, out_ref):
        gate_sum = gate_ref[...].astype(F32) + gate_far_ref[...].astype(F32)
        up_sum = up_ref[...].astype(F32) + up_far_ref[...].astype(F32)
        out_ref[...] = (gate_sum * jax.nn.sigmoid(gate_sum) * up_sum).astype(B16)

    return pl.pallas_call(
        kernel,
        name="activate",
        in_specs=[VMEM] * 4,
        out_specs=VMEM,
        out_shape=jax.ShapeDtypeStruct(gate.shape, B16),
        compiler_params=params(4),
        cost_estimate=cost(gate.size * 300, 0),
    )(gate, gate_far, up, up_far)


def deltas(gate, gate_far, up, up_far, delta, delta_far, after=()):
    count, width = gate.shape

    def kernel(gate_ref, gate_far_ref, up_ref, up_far_ref, delta_ref, delta_far_ref, *rest):
        out_ref = rest[-1]
        gate_sum = gate_ref[...].astype(F32) + gate_far_ref[...].astype(F32)
        up_sum = up_ref[...].astype(F32) + up_far_ref[...].astype(F32)
        hidden_delta = delta_ref[...].astype(F32) + delta_far_ref[...].astype(F32)
        sigmoid = jax.nn.sigmoid(gate_sum)
        out_ref[:count] = (
            hidden_delta * up_sum * sigmoid * (1.0 + gate_sum * (1.0 - sigmoid))
        ).astype(B16)
        out_ref[count:] = (hidden_delta * (gate_sum * sigmoid)).astype(B16)

    return pl.pallas_call(
        kernel,
        name="deltas",
        in_specs=[VMEM] * 6 + [ANY] * len(after),
        out_specs=VMEM,
        out_shape=jax.ShapeDtypeStruct((2 * count, width), B16),
        compiler_params=params(4),
        cost_estimate=cost(gate.size * 300, 0),
    )(gate, gate_far, up, up_far, delta, delta_far, *after)


def output_part(side, mask, weight, hidden, before=None, after=()):
    pieces = len(weight)
    count = hidden.shape[0]
    depth, width = weight[0].shape
    tile = fit(depth // 2, 512)
    step = fit(width, 256)

    def kernel(mask_ref, *rest):
        weight_refs, hidden_ref, before_ref, out_ref = rest[:pieces], rest[pieces], rest[pieces + 1], rest[-1]
        base = half_of_pair(side) * pieces * (width // BLOCK)

        def one(t, carry):
            starts = [pl.multiple_of((2 * t + n) * tile, BLOCK) for n in range(2)]
            both = jnp.concatenate(
                [
                    total(
                        contract(
                            keep_blocks(
                                weight_refs[p][pl.ds(start, tile), k : k + step],
                                lambda i, j: mask_ref[
                                    start // BLOCK + i, base + (p * width + k) // BLOCK + j
                                ],
                            ),
                            hidden_ref[:, p * width + k : p * width + k + step],
                            1,
                            1,
                        )
                        for p in range(pieces)
                        for k in range(0, width, step)
                    )
                    for start in starts
                ],
                1,
            ).T
            for n, start in enumerate(starts):
                out = both[n * count : (n + 1) * count]
                if before is not None:
                    out = out + before_ref[:, pl.ds(start, tile)]
                out_ref[:, pl.ds(start, tile)] = out
            return carry

        lax.fori_loop(0, depth // (2 * tile), one, 0)

    more = [] if before is None else [before]
    return pl.pallas_call(
        kernel,
        name="output_part",
        in_specs=[SMEM] + [VMEM] * (pieces + 1 + len(more)) + [ANY] * len(after),
        out_specs=VMEM,
        out_shape=jax.ShapeDtypeStruct((count, depth), F32),
        compiler_params=params(4),
        cost_estimate=cost(1, 1),
    )(mask, *resident(weight), hidden, *more, *after)


def input_part(side, masks, gate, up, delta, before=None, output=None, blocks=1):
    pieces = len(gate)
    count = delta.shape[0] // 2
    width, depth = gate[0].shape
    tile = fit(depth, 1024)
    step = fit(width, 256)
    rows = count // blocks

    def kernel(gate_mask_ref, up_mask_ref, *rest):
        gate_refs, up_refs, delta_ref = rest[:pieces], rest[pieces : 2 * pieces], rest[2 * pieces]
        rest = rest[2 * pieces + 1 :]
        base = half_of_pair(side) * pieces * (width // BLOCK)

        def one(t, carry):
            start = pl.multiple_of(t * tile, BLOCK)
            here = pl.ds(start, tile)
            acc = total(
                contract(
                    delta_ref[row : row + count, p * width + k : p * width + k + step],
                    keep_blocks(
                        refs[p][k : k + step, here],
                        lambda i, j: mask_ref[
                            start // BLOCK + j, base + (p * width + k) // BLOCK + i
                        ],
                    ),
                    1,
                    0,
                )
                for refs, mask_ref, row in (
                    (gate_refs, gate_mask_ref, 0),
                    (up_refs, up_mask_ref, count),
                )
                for p in range(pieces)
                for k in range(0, width, step)
            )
            if before is None:
                rest[0][:, here] = acc
            else:
                acc = (acc + rest[0][:, here]).astype(B16)
                out = rest[1][:, here].astype(B16)
                for b in range(blocks):
                    rest[2 + b][:rows, here] = out[b * rows : (b + 1) * rows]
                    rest[2 + b][rows:, here] = acc[b * rows : (b + 1) * rows]
            return carry

        lax.fori_loop(0, depth // tile, one, 0)

    if before is None:
        more, out_shape = [], [jax.ShapeDtypeStruct((count, depth), F32)]
    else:
        more = [before, output]
        out_shape = [jax.ShapeDtypeStruct((2 * rows, depth), B16)] * blocks
    return pl.pallas_call(
        kernel,
        name="input_part",
        in_specs=[SMEM] * 2 + [VMEM] * (2 * pieces + 1 + len(more)),
        out_specs=[VMEM] * len(out_shape),
        out_shape=out_shape,
        compiler_params=params(4),
        cost_estimate=cost(16 * count * depth * width * pieces, 0),
    )(masks[0].T, masks[1].T, *resident(gate), *resident(up), delta, *more)


def weight_grads(masks, joint, hidden, delta):
    parts = len(joint)
    rows, depth = joint[0].shape[0] // 2, joint[0].shape[1]
    count = parts * rows
    width = hidden[0].shape[1]
    tall = fit(width, 1024)
    wide = fit(min(width, depth), 2048)
    chunk = fit(wide, 512)
    slots = 3

    def kernel(gate_mask_ref, up_mask_ref, down_mask_ref, *rest):
        hidden_refs, delta_refs = rest[:2], rest[2:4]
        rest = rest[4:]
        joint_refs = rest[:parts]
        gate_out, up_out, down_out, ring, sems, hidden_all, turned, tokens_all, grads_turned = rest[parts:]
        for side in (OWN, FAR):
            hidden_all[side] = hidden_refs[side][...]
            for kind in range(2):
                turned[kind, side] = delta_refs[side][kind * count : (kind + 1) * count].T
        tokens_all[...] = stacked(joint_refs, slice(0, rows), slice(None))
        grads_turned[...] = stacked(joint_refs, slice(rows, None), slice(None)).T

        def copy(slot, target):
            return pltpu.make_async_copy(ring.at[slot], target, sems.at[slot])

        def tiles(done, out_ref, mask_ref, height, columns, row_tile, column_tile, left, right, place):
            across = columns // column_tile
            each = (height // row_tile) * across

            def one(n, carry):
                side = n // each
                at = n % each
                row = pl.multiple_of((at // across) * row_tile, BLOCK)
                column = pl.multiple_of((at % across) * column_tile, BLOCK)
                slot = (done + n) % slots
                to_row, to_column = place(side, row, column)
                target = out_ref.at[pl.ds(to_row, row_tile), pl.ds(to_column, column_tile)]

                def free():
                    copy(slot, target).wait()

                if done >= slots:
                    free()
                else:
                    pl.when(done + n >= slots)(free)
                lhs = left(side, row)
                for c in range(0, column_tile, chunk):
                    size = min(chunk, column_tile - c)
                    tile = contract(lhs, right(side, column, c, size), 1, 0).astype(B16)
                    tile = keep_blocks(
                        tile,
                        lambda i, j: mask_ref(to_row // BLOCK + i, (to_column + c) // BLOCK + j),
                    )
                    ring[slot, :, c : c + size] = tile
                copy(slot, target).start()
                return carry

            lax.fori_loop(0, 2 * each, one, 0)
            return done + 2 * each

        done = tiles(
            0, down_out, lambda i, j: down_mask_ref[i, j], depth, width, tall, wide,
            lambda side, row: grads_turned[pl.ds(row, tall), :],
            lambda side, column, c, size: hidden_all[side, :, pl.ds(pl.multiple_of(column + c, BLOCK), size)],
            lambda side, row, column: (row, pl.multiple_of(half_of_pair(side) * width + column, BLOCK)),
        )
        for kind, out_ref, mask in ((0, gate_out, gate_mask_ref), (1, up_out, up_mask_ref)):
            done = tiles(
                done, out_ref, lambda i, j: mask[j, i], width, depth, tall, wide,
                lambda side, row: turned[kind, side, pl.ds(row, tall), :],
                lambda side, column, c, size: tokens_all[:, pl.ds(pl.multiple_of(column + c, BLOCK), size)],
                lambda side, row, column: (pl.multiple_of(half_of_pair(side) * width + row, BLOCK), column),
            )
        for slot in range(min(slots, done)):
            copy(slot, up_out.at[pl.ds(0, tall), pl.ds(0, wide)]).wait()

    return pl.pallas_call(
        kernel,
        name="weight_grads",
        in_specs=[SMEM] * 3 + [VMEM] * (4 + parts),
        out_specs=[ANY] * 3,
        out_shape=[
            jax.ShapeDtypeStruct((2 * width, depth), B16),
            jax.ShapeDtypeStruct((2 * width, depth), B16),
            jax.ShapeDtypeStruct((depth, 2 * width), B16),
        ],
        scratch_shapes=[
            pltpu.VMEM((slots, tall, wide), B16),
            pltpu.SemaphoreType.DMA((slots,)),
            pltpu.VMEM((2, count, width), B16),
            pltpu.VMEM((2, 2, width, count), B16),
            pltpu.VMEM((count, depth), B16),
            pltpu.VMEM((depth, count), B16),
        ],
        compiler_params=params(24),
        cost_estimate=cost(0, 12 * width * depth),
    )(masks[0].T, masks[1].T, masks[2], *hidden, *delta, *joint)


def body(rows, tokens, output_grad, gate_weight, up_weight, down_weight, gate_mask, up_mask, down_mask):
    masks = (gate_mask, up_mask, down_mask)
    direct = rows <= 4
    pieces = 2 if gate_weight.shape[0] >= 2048 else 1

    def gather(array):
        if not direct:
            return list(lax.all_gather(array, "row", axis=0))
        return [array] + [
            lax.ppermute(array, "row", [(i, (i + s) % rows) for i in range(rows)])
            for s in range(1, rows)
        ]

    def swap(array, bit):
        size = lax.axis_size("col")
        return lax.ppermute(array, "col", [(i, i ^ bit) for i in range(size)])

    joint = gather(join(tokens, output_grad))
    gate_w, up_w, down_w = load(((gate_weight, 0), (up_weight, 0), (down_weight, 1)), pieces)

    gate_sent = up_forward(FAR, gate_mask, gate_w[FAR], joint)
    up_sent = up_forward(FAR, up_mask, up_w[FAR], joint)
    delta_sent = down_forward(FAR, down_mask, down_w[FAR], joint)
    gate = up_forward(OWN, gate_mask, gate_w[OWN], joint, swap(gate_sent, 1))
    gate_far = swap(gate, 2)
    up = up_forward(OWN, up_mask, up_w[OWN], joint, swap(up_sent, 1))
    up_far = swap(up, 2)
    delta = down_forward(OWN, down_mask, down_w[OWN], joint, swap(delta_sent, 1))
    delta_far = swap(delta, 2)

    hidden = activate(gate, gate_far, up, up_far)
    hidden = (hidden, swap(hidden, 1))
    out = output_part(OWN, down_mask, down_w[OWN], hidden[OWN], after=[delta])
    both = deltas(gate, gate_far, up, up_far, delta, delta_far, after=[out])
    out = output_part(FAR, down_mask, down_w[FAR], hidden[FAR], out, after=[both])
    both = (both, swap(both, 1))
    first = input_part(OWN, masks, gate_w[OWN], up_w[OWN], both[OWN])
    blocks = input_part(
        FAR, masks, gate_w[FAR], up_w[FAR], both[FAR], first[0], out, rows if direct else 1
    )
    count = tokens.shape[0]
    if direct:
        parts = [blocks[0]]
        for s in range(1, rows):
            parts.append(lax.ppermute(blocks[s], "row", [(i, (i - s) % rows) for i in range(rows)]))
        summed = total(p.astype(F32) for p in parts).astype(B16)
        output, input_grad = summed[:count], summed[count:]
    else:
        half = blocks[0].shape[0] // 2
        output, input_grad = [
            lax.psum_scatter(part, "row", scatter_dimension=0, tiled=True)
            for part in (blocks[0][:half], blocks[0][half:])
        ]
    gate_grad, up_grad, down_grad = weight_grads(masks, joint, hidden, both)
    return output, input_grad, gate_grad, up_grad, down_grad


def solution(mesh):
    rows = mesh.shape["row"]
    held = P(("member", "row"), "col")
    down_held = P(("member", "col"), "row")
    return jax.shard_map(
        functools.partial(body, rows),
        mesh=mesh,
        in_specs=(held, held, held, held, down_held, P("row", "col"), P("row", "col"), P("col", "row")),
        out_specs=(held, held, held, held, down_held),
        check_vma=False,
    )
```

```python
import functools

import jax
import jax.numpy as jnp
from jax import lax
from jax.experimental import pallas as pl
from jax.experimental.pallas import tpu as pltpu
from jax.sharding import PartitionSpec as P

B16 = jnp.bfloat16
F32 = jnp.float32
BLOCK = 128
MIB = 2**20
OWN, FAR = 0, 1
CUTS = 1

VMEM = pl.BlockSpec(memory_space=pltpu.VMEM)
SMEM = pl.BlockSpec(memory_space=pltpu.SMEM)
ANY = pl.BlockSpec(memory_space=pl.ANY)


def contract(left, right, left_dim, right_dim):
    return lax.dot_general(
        left, right, (((left_dim,), (right_dim,)), ((), ())), preferred_element_type=F32
    )


def keep_blocks(tile, kept):
    rows = []
    for i in range(tile.shape[0] // BLOCK):
        row = []
        for j in range(tile.shape[1] // BLOCK):
            block = tile[BLOCK * i : BLOCK * (i + 1), BLOCK * j : BLOCK * (j + 1)]
            row.append(jnp.where(kept(i, j) != 0, block, jnp.zeros_like(block)))
        rows.append(row[0] if len(row) == 1 else jnp.concatenate(row, 1))
    return rows[0] if len(rows) == 1 else jnp.concatenate(rows, 0)


def stacked(refs, rows, span):
    parts = [ref[rows, span] for ref in refs]
    return parts[0] if len(parts) == 1 else jnp.concatenate(parts, 0)


def half_of_pair(side):
    return (lax.axis_index("col") + side) % 2


def total(parts):
    return functools.reduce(lambda a, b: a + b, parts)


def fit(size, most):
    return size if size < most else most


def params(mib):
    return pltpu.CompilerParams(vmem_limit_bytes=mib * MIB)


def cost(flops, read):
    return pl.CostEstimate(flops=flops, bytes_accessed=read, transcendentals=0)


def resident(arrays):
    return [pltpu.with_memory_space_constraint(a, pltpu.VMEM) for a in arrays]


def piece_shapes(weight, dim, pieces):
    shape = list(weight.shape)
    shape[dim] //= 2 * pieces
    return [tuple(shape)] * pieces


def piece_copies(source_ref, dim, side, out_refs, sems):
    copies = []
    for p, out_ref in enumerate(out_refs):
        height, size = out_ref.shape[0] // CUTS, out_ref.shape[dim]
        first = pl.multiple_of((half_of_pair(side) * len(out_refs) + p) * size, BLOCK)
        for cut in range(CUTS):
            here = pl.ds(cut * height, height)
            if dim == 0:
                source = source_ref.at[pl.ds(first + cut * height, height)]
            else:
                source = source_ref.at[here, pl.ds(first, size)]
            copies.append(
                pltpu.make_async_copy(source, out_ref.at[here], sems.at[p * CUTS + cut])
            )
    return copies


def join(top, bottom):
    height, width = top.shape

    def kernel(top_ref, bottom_ref, out_ref, sems):
        copies = [
            pltpu.make_async_copy(ref, out_ref.at[pl.ds(n * height, height)], sems.at[n])
            for n, ref in enumerate((top_ref, bottom_ref))
        ]
        for copy in copies:
            copy.start()
        for copy in copies:
            copy.wait()

    return pl.pallas_call(
        kernel,
        name="join",
        in_specs=[ANY] * 2,
        out_specs=VMEM,
        out_shape=jax.ShapeDtypeStruct((2 * height, width), top.dtype),
        scratch_shapes=[pltpu.SemaphoreType.DMA((2,))],
        compiler_params=params(1),
    )(in_hbm(top), in_hbm(bottom))


def in_hbm(array):
    return pltpu.with_memory_space_constraint(array, pltpu.HBM)


def load(items, pieces, after=()):
    count = len(items)
    shapes = [s for weight, dim in items for s in piece_shapes(weight, dim, pieces) * 2]

    def kernel(*refs):
        outs, sems = refs[count + len(after) : -1], refs[-1]
        copies = []
        for n, (_, dim) in enumerate(items):
            for side in (OWN, FAR):
                at = (2 * n + side) * pieces
                copies += piece_copies(
                    refs[n], dim, side, outs[at : at + pieces],
                    sems.at[pl.ds(at * CUTS, pieces * CUTS)],
                )
        for copy in copies:
            copy.start()
        for copy in copies:
            copy.wait()

    loaded = pl.pallas_call(
        kernel,
        name="load",
        in_specs=[ANY] * (count + len(after)),
        out_specs=[VMEM] * len(shapes),
        out_shape=[pltpu.VMEM(s, B16) for s in shapes],
        scratch_shapes=[pltpu.SemaphoreType.DMA((len(shapes) * CUTS,))],
        compiler_params=params(1),
        cost_estimate=cost(1, 1) if after else cost(0, sum(w.size * 2 for w, _ in items)),
    )(*[in_hbm(w) for w, _ in items], *after)
    return [
        [loaded[(2 * n + side) * pieces : (2 * n + side + 1) * pieces] for side in (OWN, FAR)]
        for n in range(count)
    ]


def down_forward(side, mask, weight, grads, recv=None, after=()):
    pieces, parts = len(weight), len(grads)
    rows, depth = grads[0].shape[0] // 2, grads[0].shape[1]
    tokens = parts * rows
    width = weight[0].shape[1]
    tile = fit(width, 1024)
    step = fit(depth, 256)

    def kernel(mask_ref, *rest):
        weight_refs, grads_refs = rest[:pieces], rest[pieces : pieces + parts]
        recv_ref, out_ref = rest[pieces + parts], rest[-1]
        for p in range(pieces):
            base = (half_of_pair(side) * pieces + p) * (width // BLOCK)

            def one(t, carry):
                start = pl.multiple_of(t * tile, BLOCK)
                here = pl.ds(pl.multiple_of(p * width + t * tile, BLOCK), tile)
                acc = total(
                    contract(
                        stacked(grads_refs, slice(rows, None), slice(k, k + step)),
                        keep_blocks(
                            weight_refs[p][k : k + step, pl.ds(start, tile)],
                            lambda i, j: mask_ref[k // BLOCK + i, base + start // BLOCK + j],
                        ),
                        1,
                        0,
                    )
                    for k in range(0, depth, step)
                )
                if recv is not None:
                    acc = acc + recv_ref[:, here].astype(F32)
                out_ref[:, here] = acc.astype(B16)
                return carry

            lax.fori_loop(0, width // tile, one, 0)

    more = [] if recv is None else [recv]
    return pl.pallas_call(
        kernel,
        name="down_forward",
        in_specs=[SMEM] + [VMEM] * (pieces + parts + len(more)) + [ANY] * len(after),
        out_specs=VMEM,
        out_shape=jax.ShapeDtypeStruct((tokens, pieces * width), B16),
        compiler_params=params(4),
        cost_estimate=cost(1, 1),
    )(mask, *resident(weight), *grads, *more, *after)


def up_forward(side, mask, weight, tokens, recv=None, after=()):
    pieces, parts = len(weight), len(tokens)
    rows, depth = tokens[0].shape[0] // 2, tokens[0].shape[1]
    count = parts * rows
    width = weight[0].shape[0]
    tile = fit(width // 2, 512)
    step = fit(depth, 256)

    def kernel(mask_ref, *rest):
        weight_refs, tokens_refs = rest[:pieces], rest[pieces : pieces + parts]
        recv_ref, out_ref = rest[pieces + parts], rest[-1]
        for p in range(pieces):
            base = (half_of_pair(side) * pieces + p) * (width // BLOCK)

            def one(t, carry):
                starts = [pl.multiple_of((2 * t + n) * tile, BLOCK) for n in range(2)]
                both = jnp.concatenate(
                    [
                        total(
                            contract(
                                keep_blocks(
                                    weight_refs[p][pl.ds(start, tile), k : k + step],
                                    lambda i, j: mask_ref[k // BLOCK + j, base + start // BLOCK + i],
                                ),
                                stacked(tokens_refs, slice(0, rows), slice(k, k + step)),
                                1,
                                1,
                            )
                            for k in range(0, depth, step)
                        )
                        for start in starts
                    ],
                    1,
                ).T
                for n in range(2):
                    here = pl.ds(pl.multiple_of(p * width + (2 * t + n) * tile, BLOCK), tile)
                    out = both[n * count : (n + 1) * count]
                    if recv is not None:
                        out = out + recv_ref[:, here].astype(F32)
                    out_ref[:, here] = out.astype(B16)
                return carry

            lax.fori_loop(0, width // (2 * tile), one, 0)

    more = [] if recv is None else [recv]
    return pl.pallas_call(
        kernel,
        name="up_forward",
        in_specs=[SMEM] + [VMEM] * (pieces + parts + len(more)) + [ANY] * len(after),
        out_specs=VMEM,
        out_shape=jax.ShapeDtypeStruct((count, pieces * width), B16),
        compiler_params=params(4),
        cost_estimate=cost(1, 1),
    )(mask.T, *resident(weight), *tokens, *more, *after)


def activate(gate, gate_far, up, up_far, after=()):
    def kernel(gate_ref, gate_far_ref, up_ref, up_far_ref, *rest):
        out_ref = rest[-1]
        gate_sum = gate_ref[...].astype(F32) + gate_far_ref[...].astype(F32)
        up_sum = up_ref[...].astype(F32) + up_far_ref[...].astype(F32)
        out_ref[...] = (gate_sum * jax.nn.sigmoid(gate_sum) * up_sum).astype(B16)

    return pl.pallas_call(
        kernel,
        name="activate",
        in_specs=[VMEM] * 4 + [ANY] * len(after),
        out_specs=VMEM,
        out_shape=jax.ShapeDtypeStruct(gate.shape, B16),
        compiler_params=params(4),
        cost_estimate=cost(gate.size * 300, 0),
    )(gate, gate_far, up, up_far, *after)


def deltas(gate, gate_far, up, up_far, delta, delta_far, after=()):
    count, width = gate.shape

    def kernel(gate_ref, gate_far_ref, up_ref, up_far_ref, delta_ref, delta_far_ref, *rest):
        out_ref = rest[-1]
        gate_sum = gate_ref[...].astype(F32) + gate_far_ref[...].astype(F32)
        up_sum = up_ref[...].astype(F32) + up_far_ref[...].astype(F32)
        hidden_delta = delta_ref[...].astype(F32) + delta_far_ref[...].astype(F32)
        sigmoid = jax.nn.sigmoid(gate_sum)
        out_ref[:count] = (
            hidden_delta * up_sum * sigmoid * (1.0 + gate_sum * (1.0 - sigmoid))
        ).astype(B16)
        out_ref[count:] = (hidden_delta * (gate_sum * sigmoid)).astype(B16)

    return pl.pallas_call(
        kernel,
        name="deltas",
        in_specs=[VMEM] * 6 + [ANY] * len(after),
        out_specs=VMEM,
        out_shape=jax.ShapeDtypeStruct((2 * count, width), B16),
        compiler_params=params(4),
        cost_estimate=cost(gate.size * 300, 0),
    )(gate, gate_far, up, up_far, delta, delta_far, *after)


def output_part(side, mask, weight, hidden, before=None, after=()):
    pieces = len(weight)
    count = hidden.shape[0]
    depth, width = weight[0].shape
    tile = fit(depth // 2, 512)
    step = fit(width, 256)

    def kernel(mask_ref, *rest):
        weight_refs, hidden_ref, before_ref, out_ref = rest[:pieces], rest[pieces], rest[pieces + 1], rest[-1]
        base = half_of_pair(side) * pieces * (width // BLOCK)

        def one(t, carry):
            starts = [pl.multiple_of((2 * t + n) * tile, BLOCK) for n in range(2)]
            both = jnp.concatenate(
                [
                    total(
                        contract(
                            keep_blocks(
                                weight_refs[p][pl.ds(start, tile), k : k + step],
                                lambda i, j: mask_ref[
                                    start // BLOCK + i, base + (p * width + k) // BLOCK + j
                                ],
                            ),
                            hidden_ref[:, p * width + k : p * width + k + step],
                            1,
                            1,
                        )
                        for p in range(pieces)
                        for k in range(0, width, step)
                    )
                    for start in starts
                ],
                1,
            ).T
            for n, start in enumerate(starts):
                out = both[n * count : (n + 1) * count]
                if before is not None:
                    out = out + before_ref[:, pl.ds(start, tile)]
                out_ref[:, pl.ds(start, tile)] = out
            return carry

        lax.fori_loop(0, depth // (2 * tile), one, 0)

    more = [] if before is None else [before]
    return pl.pallas_call(
        kernel,
        name="output_part",
        in_specs=[SMEM] + [VMEM] * (pieces + 1 + len(more)) + [ANY] * len(after),
        out_specs=VMEM,
        out_shape=jax.ShapeDtypeStruct((count, depth), F32),
        compiler_params=params(4),
        cost_estimate=cost(1, 1),
    )(mask, *resident(weight), hidden, *more, *after)


def input_part(side, masks, gate, up, delta, before=None, output=None, blocks=1):
    pieces = len(gate)
    count = delta.shape[0] // 2
    width, depth = gate[0].shape
    tile = fit(depth, 1024)
    step = fit(width, 256)
    rows = count // blocks

    def kernel(gate_mask_ref, up_mask_ref, *rest):
        gate_refs, up_refs, delta_ref = rest[:pieces], rest[pieces : 2 * pieces], rest[2 * pieces]
        rest = rest[2 * pieces + 1 :]
        base = half_of_pair(side) * pieces * (width // BLOCK)

        def one(t, carry):
            start = pl.multiple_of(t * tile, BLOCK)
            here = pl.ds(start, tile)
            acc = total(
                contract(
                    delta_ref[row : row + count, p * width + k : p * width + k + step],
                    keep_blocks(
                        refs[p][k : k + step, here],
                        lambda i, j: mask_ref[
                            start // BLOCK + j, base + (p * width + k) // BLOCK + i
                        ],
                    ),
                    1,
                    0,
                )
                for refs, mask_ref, row in (
                    (gate_refs, gate_mask_ref, 0),
                    (up_refs, up_mask_ref, count),
                )
                for p in range(pieces)
                for k in range(0, width, step)
            )
            if before is None:
                rest[0][:, here] = acc
            else:
                acc = (acc + rest[0][:, here]).astype(B16)
                out = rest[1][:, here].astype(B16)
                for b in range(blocks):
                    rest[2 + b][:rows, here] = out[b * rows : (b + 1) * rows]
                    rest[2 + b][rows:, here] = acc[b * rows : (b + 1) * rows]
            return carry

        lax.fori_loop(0, depth // tile, one, 0)

    if before is None:
        more, out_shape = [], [jax.ShapeDtypeStruct((count, depth), F32)]
    else:
        more = [before, output]
        out_shape = [jax.ShapeDtypeStruct((2 * rows, depth), B16)] * blocks
    return pl.pallas_call(
        kernel,
        name="input_part",
        in_specs=[SMEM] * 2 + [VMEM] * (2 * pieces + 1 + len(more)),
        out_specs=[VMEM] * len(out_shape),
        out_shape=out_shape,
        compiler_params=params(4),
        cost_estimate=cost(16 * count * depth * width * pieces, 0),
    )(masks[0].T, masks[1].T, *resident(gate), *resident(up), delta, *more)


def weight_grads(masks, joint, hidden, delta):
    parts = len(joint)
    rows, depth = joint[0].shape[0] // 2, joint[0].shape[1]
    count = parts * rows
    width = hidden[0].shape[1]
    tall = fit(width, 1024)
    wide = fit(min(width, depth), 2048)
    chunk = fit(wide, 512)
    slots = 3

    def kernel(gate_mask_ref, up_mask_ref, down_mask_ref, *rest):
        hidden_refs, delta_refs = rest[:2], rest[2:4]
        rest = rest[4:]
        joint_refs = rest[:parts]
        gate_out, up_out, down_out, ring, sems, hidden_all, turned, tokens_all, grads_turned = rest[parts:]
        for side in (OWN, FAR):
            hidden_all[side] = hidden_refs[side][...]
            for kind in range(2):
                turned[kind, side] = delta_refs[side][kind * count : (kind + 1) * count].T
        tokens_all[...] = stacked(joint_refs, slice(0, rows), slice(None))
        grads_turned[...] = stacked(joint_refs, slice(rows, None), slice(None)).T

        def copy(slot, target):
            return pltpu.make_async_copy(ring.at[slot], target, sems.at[slot])

        def tiles(done, out_ref, mask_ref, height, columns, row_tile, column_tile, left, right, place):
            across = columns // column_tile
            each = (height // row_tile) * across

            def one(n, carry):
                side = n // each
                at = n % each
                row = pl.multiple_of((at // across) * row_tile, BLOCK)
                column = pl.multiple_of((at % across) * column_tile, BLOCK)
                slot = (done + n) % slots
                to_row, to_column = place(side, row, column)
                target = out_ref.at[pl.ds(to_row, row_tile), pl.ds(to_column, column_tile)]

                def free():
                    copy(slot, target).wait()

                if done >= slots:
                    free()
                else:
                    pl.when(done + n >= slots)(free)
                lhs = left(side, row)
                for c in range(0, column_tile, chunk):
                    size = min(chunk, column_tile - c)
                    tile = contract(lhs, right(side, column, c, size), 1, 0).astype(B16)
                    tile = keep_blocks(
                        tile,
                        lambda i, j: mask_ref(to_row // BLOCK + i, (to_column + c) // BLOCK + j),
                    )
                    ring[slot, :, c : c + size] = tile
                copy(slot, target).start()
                return carry

            lax.fori_loop(0, 2 * each, one, 0)
            return done + 2 * each

        done = tiles(
            0, down_out, lambda i, j: down_mask_ref[i, j], depth, width, tall, wide,
            lambda side, row: grads_turned[pl.ds(row, tall), :],
            lambda side, column, c, size: hidden_all[side, :, pl.ds(pl.multiple_of(column + c, BLOCK), size)],
            lambda side, row, column: (row, pl.multiple_of(half_of_pair(side) * width + column, BLOCK)),
        )
        for kind, out_ref, mask in ((0, gate_out, gate_mask_ref), (1, up_out, up_mask_ref)):
            done = tiles(
                done, out_ref, lambda i, j: mask[j, i], width, depth, tall, wide,
                lambda side, row: turned[kind, side, pl.ds(row, tall), :],
                lambda side, column, c, size: tokens_all[:, pl.ds(pl.multiple_of(column + c, BLOCK), size)],
                lambda side, row, column: (pl.multiple_of(half_of_pair(side) * width + row, BLOCK), column),
            )
        for slot in range(min(slots, done)):
            copy(slot, up_out.at[pl.ds(0, tall), pl.ds(0, wide)]).wait()

    return pl.pallas_call(
        kernel,
        name="weight_grads",
        in_specs=[SMEM] * 3 + [VMEM] * (4 + parts),
        out_specs=[ANY] * 3,
        out_shape=[
            jax.ShapeDtypeStruct((2 * width, depth), B16),
            jax.ShapeDtypeStruct((2 * width, depth), B16),
            jax.ShapeDtypeStruct((depth, 2 * width), B16),
        ],
        scratch_shapes=[
            pltpu.VMEM((slots, tall, wide), B16),
            pltpu.SemaphoreType.DMA((slots,)),
            pltpu.VMEM((2, count, width), B16),
            pltpu.VMEM((2, 2, width, count), B16),
            pltpu.VMEM((count, depth), B16),
            pltpu.VMEM((depth, count), B16),
        ],
        compiler_params=params(24),
        cost_estimate=cost(0, 12 * width * depth),
    )(masks[0].T, masks[1].T, masks[2], *hidden, *delta, *joint)


def body(rows, tokens, output_grad, gate_weight, up_weight, down_weight, gate_mask, up_mask, down_mask):
    masks = (gate_mask, up_mask, down_mask)
    direct = rows <= 4
    pieces = 2 if gate_weight.shape[0] >= 2048 else 1

    def gather(array):
        if not direct:
            return list(lax.all_gather(array, "row", axis=0))
        return [array] + [
            lax.ppermute(array, "row", [(i, (i + s) % rows) for i in range(rows)])
            for s in range(1, rows)
        ]

    def swap(array, bit):
        size = lax.axis_size("col")
        return lax.ppermute(array, "col", [(i, i ^ bit) for i in range(size)])

    joint = gather(join(tokens, output_grad))
    gate_w, up_w = load(((gate_weight, 0), (up_weight, 0)), pieces)

    gate_sent = up_forward(FAR, gate_mask, gate_w[FAR], joint)
    up_sent = up_forward(FAR, up_mask, up_w[FAR], joint, after=[gate_sent])
    gate = up_forward(OWN, gate_mask, gate_w[OWN], joint, swap(gate_sent, 1), after=[up_sent])
    gate_far = swap(gate, 2)
    up = up_forward(OWN, up_mask, up_w[OWN], joint, swap(up_sent, 1), after=[gate])
    up_far = swap(up, 2)
    (down_w,) = load(((down_weight, 1),), pieces, after=[up])
    delta_sent = down_forward(FAR, down_mask, down_w[FAR], joint, after=[gate_far])
    hidden = activate(gate, gate_far, up, up_far, after=[delta_sent])
    hidden = (hidden, swap(hidden, 1))
    delta = down_forward(OWN, down_mask, down_w[OWN], joint, swap(delta_sent, 1), after=[hidden[OWN]])
    delta_far = swap(delta, 2)

    out = output_part(OWN, down_mask, down_w[OWN], hidden[OWN], after=[delta])
    out = output_part(FAR, down_mask, down_w[FAR], hidden[FAR], out)
    both = deltas(gate, gate_far, up, up_far, delta, delta_far, after=[out])
    both = (both, swap(both, 1))
    first = input_part(OWN, masks, gate_w[OWN], up_w[OWN], both[OWN])
    blocks = input_part(
        FAR, masks, gate_w[FAR], up_w[FAR], both[FAR], first[0], out, rows if direct else 1
    )
    count = tokens.shape[0]
    if direct:
        parts = [blocks[0]]
        for s in range(1, rows):
            parts.append(lax.ppermute(blocks[s], "row", [(i, (i - s) % rows) for i in range(rows)]))
        summed = total(p.astype(F32) for p in parts).astype(B16)
        output, input_grad = summed[:count], summed[count:]
    else:
        half = blocks[0].shape[0] // 2
        output, input_grad = [
            lax.psum_scatter(part, "row", scatter_dimension=0, tiled=True)
            for part in (blocks[0][:half], blocks[0][half:])
        ]
    gate_grad, up_grad, down_grad = weight_grads(masks, joint, hidden, both)
    return output, input_grad, gate_grad, up_grad, down_grad


def solution(mesh):
    rows = mesh.shape["row"]
    held = P(("member", "row"), "col")
    down_held = P(("member", "col"), "row")
    return jax.shard_map(
        functools.partial(body, rows),
        mesh=mesh,
        in_specs=(held, held, held, held, down_held, P("row", "col"), P("row", "col"), P("col", "row")),
        out_specs=(held, held, held, held, down_held),
        check_vma=False,
    )
```
